32 devices in a mesh: row: 4 (over y, x), col: 8 (over z, core).
Axes of the slice: x: 2, y: 2, z: 4, core: 2. Of those that a mesh axis runs over, the one named last changes fastest.
Arguments:
- pair: bfloat16 [448, 448, 128], P('row', 'col'), may hold values from -6 to 6
- pair_mask: int32 [448, 448], P('row', 'col'), may hold values 0 or 1
- ln_in_gain: float32 [128], replicated, may hold values from 0.1 to 1.9
- proj_ab: bfloat16 [128, 512], replicated, may hold values from -0.5 to 0.5
- gate_weight: bfloat16 [128, 128], replicated, may hold values from -0.5 to 0.5
- ln_out_gain: float32 [128], replicated, may hold values from 0.1 to 1.9
- out_weight: bfloat16 [128, 128], replicated, may hold values from -0.5 to 0.5
Outputs:
- update: bfloat16 [448, 448, 128], P('row', 'col')
The draws below stay inside these ranges and needn't reach their ends.
All inputs are finite; a program needn't handle non-finite values. No bound on the sum of `pair_mask` on one device may be relied on, other than what follows from the above.
Results may differ from the reference program's by a relative error of at most 0.008.
Values may be sent and summed in bfloat16 or wider, within the bound.
A program may use at most 192 MiB of HBM per device.

```python
import jax
import jax.numpy as jnp
from jax import lax

CH = 128
HID = 128
N = 448
N_ROW = 4


def with_ends(result, own_key, low, high):
    spot = [jax.random.randint(jax.random.fold_in(own_key, axis), (), 0, length) for axis, length in enumerate(result.shape)]
    longest = result.shape.index(max(result.shape))
    neighbour = spot[:longest] + [(spot[longest] + 1) % result.shape[longest]] + spot[longest + 1:]
    return result.at[tuple(spot)].set(low).at[tuple(neighbour)].set(high)


def block_scale(stream_key, shape, shards, low, largest):
    factor_of = 1.0
    for axis_at, parts in shards:
        heights = jax.random.uniform(jax.random.fold_in(jax.random.fold_in(stream_key, 6), axis_at), (parts,), jnp.float32, low / len(shards), largest / len(shards))
        factor_of = factor_of * jnp.repeat(jnp.exp(heights), shape[axis_at] // parts).reshape((-1,) + (1,) * (len(shape) - 1 - axis_at))
    return factor_of


def gaussian(stream_key, dims, deviation, limit, cuts=(), dtype=jnp.bfloat16):
    drawn = jax.random.normal(stream_key, dims, jnp.float32) * deviation
    if len(cuts) > 0:
        drawn = block_scale(stream_key, dims, cuts, -0.22, 0.18) * drawn
    return jnp.clip(drawn, min=-limit, max=limit).astype(dtype)


def setup_inputs(seed: int = 0) -> dict:
    streams_of = jax.random.split(jax.random.key(seed), 8)
    return {
        "pair": gaussian(streams_of[0], (N, N, CH), 1.0, 6.0, ((0, 4), (1, 8))),
        "pair_mask": with_ends((jax.random.randint(streams_of[1], (N, N), 0, 8) < 7).astype(jnp.int32), jax.random.fold_in(streams_of[1], 1), 0, 1),
        "ln_in_gain": jnp.clip(1.0 + 0.18 * jax.random.normal(streams_of[2], (CH,), jnp.float32), 0.1, 1.9),
        "proj_ab": gaussian(streams_of[3], (CH, 4 * HID), CH ** -0.5, 0.5),
        "gate_weight": gaussian(streams_of[4], (CH, CH), CH ** -0.5, 0.5),
        "ln_out_gain": jnp.clip(1.0 + 0.18 * jax.random.normal(streams_of[5], (HID,), jnp.float32), 0.1, 1.9),
        "out_weight": gaussian(streams_of[6], (HID, CH), HID ** -0.5, 0.5),
    }


EPS = 1e-05

def layer_norm(values, gain):
    values = values.astype(jnp.float32)
    middle = lax.optimization_barrier(jnp.mean(values, axis=-1, keepdims=True))
    centred = values - middle
    spread = lax.optimization_barrier(jnp.mean(centred * centred, axis=-1, keepdims=True))
    return centred * lax.rsqrt(spread + EPS) * gain.astype(jnp.float32)

def reference(pair, pair_mask, ln_in_gain, proj_ab, gate_weight, ln_out_gain, out_weight):
    span = N // N_ROW
    blocks = pair.reshape(N_ROW, span, N, CH)
    mask_blocks = pair_mask.reshape(N_ROW, span, N)

    def make(items):
        block, mask_block = items
        normed = layer_norm(block, ln_in_gain).astype(jnp.bfloat16)
        projected = jnp.dot(normed.reshape(-1, CH), proj_ab, preferred_element_type=jnp.float32)
        projected = projected.reshape(span, N, 4 * HID)
        weight = mask_block.astype(jnp.float32)[..., None]
        left = jax.nn.sigmoid(projected[..., 0:HID]) * projected[..., HID:2 * HID] * weight
        right = jax.nn.sigmoid(projected[..., 2 * HID:3 * HID]) * projected[..., 3 * HID:4 * HID] * weight
        return (left.astype(jnp.bfloat16), right.astype(jnp.bfloat16), normed)
    left, right, normed = lax.map(make, (blocks, mask_blocks))
    left = left.reshape(N, N, HID)
    right_wide = right.reshape(N, N, HID).astype(jnp.float32)
    left_cols = left.reshape(N, N_ROW, span, HID).transpose(1, 0, 2, 3)

    def finish(items):
        panel, normed_block = items
        triangle = jnp.einsum('kih,kjh->ijh', panel.astype(jnp.float32), right_wide)
        tri_normed = layer_norm(triangle, ln_out_gain).astype(jnp.bfloat16)
        gate = jax.nn.sigmoid(jnp.dot(normed_block.reshape(-1, CH), gate_weight, preferred_element_type=jnp.float32))
        mixed = jnp.dot(tri_normed.reshape(-1, HID), out_weight, preferred_element_type=jnp.float32)
        return (gate * mixed).astype(jnp.bfloat16).reshape(span, N, CH)
    update = lax.map(finish, (left_cols, normed))
    return update.reshape(N, N, CH)
```

```python
import jax
import jax.numpy as jnp
from jax import lax
from jax.sharding import PartitionSpec as P

EPS = 1e-05
AXES = ("row", "col")


def layer_norm(values, gain, axis):
    values = values.astype(jnp.float32)
    middle = jnp.mean(values, axis=axis, keepdims=True)
    centred = values - middle
    spread = jnp.mean(centred * centred, axis=axis, keepdims=True)
    return centred * lax.rsqrt(spread + EPS) * gain


def shards(pair, pair_mask, ln_in_gain, proj_ab, gate_weight, ln_out_gain, out_weight):
    rows_here, cols_here, channels = pair.shape
    hidden = out_weight.shape[0]
    tokens = rows_here * cols_here
    n_row, n_col = lax.axis_size("row"), lax.axis_size("col")
    devices = n_row * n_col
    part = hidden // devices
    ratio = n_col // n_row
    normed = layer_norm(pair, ln_in_gain, -1).astype(jnp.bfloat16).reshape(tokens, channels)
    projected = jnp.einsum("tc,ch->ht", normed, proj_ab, preferred_element_type=jnp.float32)
    weight = pair_mask.astype(jnp.float32).reshape(1, tokens)
    left = jax.nn.sigmoid(projected[0:hidden]) * projected[hidden : 2 * hidden] * weight
    right = jax.nn.sigmoid(projected[2 * hidden : 3 * hidden]) * projected[3 * hidden :] * weight
    both = jnp.stack([left.reshape(devices, part, tokens), right.reshape(devices, part, tokens)], axis=1)
    both = both.astype(jnp.bfloat16).reshape(devices, 2 * part, tokens)
    both = lax.all_to_all(both, AXES, 0, 0)
    both = both.reshape(n_row, n_col, 2, part, rows_here, cols_here)
    both = both.transpose(2, 3, 0, 4, 1, 5).reshape(2, part, n_row * rows_here, n_col * cols_here)
    triangle = jnp.einsum("hki,hkj->hij", both[0], both[1], preferred_element_type=jnp.float32)
    triangle = triangle.astype(jnp.bfloat16).reshape(part, n_row, rows_here, n_col, cols_here)
    triangle = triangle.transpose(1, 3, 0, 2, 4).reshape(devices, part, tokens)
    triangle = lax.all_to_all(triangle, AXES, 0, 0).reshape(hidden, tokens)
    tri_normed = layer_norm(triangle, ln_out_gain[:, None], 0).astype(jnp.bfloat16)
    gate = jax.nn.sigmoid(jnp.dot(normed, gate_weight, preferred_element_type=jnp.float32))
    mixed = jnp.einsum("ht,hc->tc", tri_normed, out_weight, preferred_element_type=jnp.float32)
    return (gate * mixed).astype(jnp.bfloat16).reshape(rows_here, cols_here, channels)


def solution(mesh):
    in_specs = (P("row", "col", None), P("row", "col"), P(), P(), P(), P(), P())
    out_specs = P("row", "col", None)
    return jax.shard_map(shards, mesh=mesh, in_specs=in_specs, out_specs=out_specs, check_vma=False)
```

```python
import functools

import jax
import jax.numpy as jnp
from jax import lax
from jax.experimental import pallas as pl
from jax.experimental.pallas import tpu as pltpu
from jax.sharding import PartitionSpec as P

EPS = 1e-05
LANES = 128
VMEM_LIMIT = 56 * 1024 * 1024
VMEM = pl.BlockSpec(memory_space=pltpu.VMEM)
ANY = pl.BlockSpec(memory_space=pl.ANY)


def chunks(length, size):
    return [(at, min(at + size, length)) for at in range(0, length, size)]


def pad_rows(values, to):
    short = to - values.shape[-2]
    if short == 0:
        return values
    shape = values.shape[:-2] + (short, values.shape[-1])
    return jnp.concatenate([values, jnp.zeros(shape, values.dtype)], axis=-2)


def layer_norm(values, gain, axis):
    middle = jnp.mean(values, axis=axis, keepdims=True)
    centred = values - middle
    spread = jnp.mean(centred * centred, axis=axis, keepdims=True)
    return centred * lax.rsqrt(spread + EPS) * gain


def operands_kernel(pair_ref, mask_ref, gain_ref, gates_ref, values_ref, normed_ref, out_ref):
    cols, padded = out_ref.shape[1], out_ref.shape[2]
    for low, high in chunks(cols, 8):
        normed = layer_norm(pair_ref[:, low:high, :].astype(jnp.float32), gain_ref[...], -1)
        normed_ref[:, low:high, :] = normed.astype(jnp.bfloat16)
        turned = pad_rows(jnp.transpose(normed, (1, 0, 2)), padded).astype(jnp.bfloat16)
        mine = []
        for at in range(high - low):
            turn = (((1,), (1,)), ((), ()))
            gates = lax.dot_general(gates_ref[...], turned[at], turn, preferred_element_type=jnp.float32)
            values = lax.dot_general(values_ref[...], turned[at], turn, preferred_element_type=jnp.float32)
            mine.append(jax.nn.sigmoid(gates) * values * mask_ref[low + at : low + at + 1, :])
        out_ref[:, low:high, :] = jnp.transpose(jnp.stack(mine), (1, 0, 2)).astype(jnp.bfloat16)


def exchange_kernel(
    n_row, n_col, rows, send_ref, out_ref, held, product, send_sem, recv_sem, back_sem, land_sem, own_sem
):
    part, _, _, cols, padded = held.shape
    devices = n_row * n_col
    row, col = lax.axis_index("row"), lax.axis_index("col")
    me = row * n_col + col

    def place(offset):
        other = lax.rem(me + offset, devices)
        return other, (other // n_col, lax.rem(other, n_col))

    barrier = pltpu.get_barrier_semaphore()

    def greet(offset, carry):
        pl.semaphore_signal(barrier, inc=1, device_id=place(offset)[1], device_id_type=pl.DeviceIdType.MESH)
        return carry

    lax.fori_loop(1, devices, greet, 0)
    pl.semaphore_wait(barrier, devices - 1)

    def scatter(h):
        pltpu.make_async_copy(send_ref.at[h, me], held.at[h, me], own_sem.at[h]).start()

        def one(offset, carry):
            other, device = place(offset)
            pltpu.make_async_remote_copy(
                src_ref=send_ref.at[h, other],
                dst_ref=held.at[h, me],
                send_sem=send_sem.at[h],
                recv_sem=recv_sem.at[h],
                device_id=device,
                device_id_type=pl.DeviceIdType.MESH,
            ).start()
            return carry

        lax.fori_loop(1, devices, one, 0)

    for h in range(part):
        scatter(h)

    def wait_others(ref, sem):
        some = ref.at[pl.ds(0, devices - 1)]
        pltpu.make_async_copy(some, some, sem).wait()

    def channel(h, carry):
        wait_others(held.at[h], recv_sem.at[h])
        pltpu.make_async_copy(send_ref.at[h, me], held.at[h, me], own_sem.at[h]).wait()
        sides = []
        for side in range(2):
            pieces = [
                held[h, at * n_col : (at + 1) * n_col, side].reshape(n_col * cols, padded) for at in range(n_row)
            ]
            sides.append(jnp.concatenate(pieces, axis=1))
        left, right = sides
        for at in range(n_row):
            panel = pad_rows(left[at * rows : (at + 1) * rows], padded)
            tri = lax.dot_general(right, panel, (((1,), (1,)), ((), ())), preferred_element_type=jnp.float32)
            product[h, at * n_col : (at + 1) * n_col] = tri.reshape(n_col, cols, padded).astype(jnp.bfloat16)
        pltpu.make_async_copy(product.at[h, me], out_ref.at[h, me], own_sem.at[h]).start()

        def one(offset, inner):
            other, device = place(offset)
            pltpu.make_async_remote_copy(
                src_ref=product.at[h, other],
                dst_ref=out_ref.at[h, me],
                send_sem=back_sem.at[h],
                recv_sem=land_sem.at[h],
                device_id=device,
                device_id_type=pl.DeviceIdType.MESH,
            ).start()
            return inner

        lax.fori_loop(1, devices, one, 0)
        return carry

    lax.fori_loop(0, part, channel, 0)

    def finish(h, carry):
        wait_others(out_ref.at[h], land_sem.at[h])
        pltpu.make_async_copy(product.at[h, me], out_ref.at[h, me], own_sem.at[h]).wait()
        wait_others(held.at[h], send_sem.at[h])
        wait_others(product.at[h], back_sem.at[h])
        return carry

    lax.fori_loop(0, part, finish, 0)


def update_kernel(tri_ref, normed_ref, gain_ref, gate_ref, weight_ref, out_ref):
    rows, cols, channels = normed_ref.shape
    for low, high in chunks(cols, 8):
        tri = layer_norm(tri_ref[:, low:high, :].astype(jnp.float32), gain_ref[...], 0)
        tri = jnp.transpose(tri, (1, 0, 2)).astype(jnp.bfloat16)
        mixed = []
        for at in range(high - low):
            turn = (((0,), (0,)), ((), ()))
            mixed.append(lax.dot_general(tri[at], weight_ref[...], turn, preferred_element_type=jnp.float32)[:rows])
        mixed = jnp.transpose(jnp.stack(mixed), (1, 0, 2))
        normed = normed_ref[:, low:high, :].astype(jnp.float32).reshape(rows * (high - low), channels)
        gate = jnp.dot(normed.astype(jnp.bfloat16), gate_ref[...], preferred_element_type=jnp.float32)
        gate = jax.nn.sigmoid(gate).reshape(rows, high - low, channels)
        out_ref[:, low:high, :] = (gate * mixed).astype(jnp.bfloat16)


def shards(pair, pair_mask, ln_in_gain, proj_ab, gate_weight, ln_out_gain, out_weight):
    rows, cols, channels = pair.shape
    hidden = out_weight.shape[0]
    n_row, n_col = lax.axis_size("row"), lax.axis_size("col")
    devices = n_row * n_col
    part = hidden // devices
    padded = -(-rows // LANES) * LANES
    plain = pltpu.CompilerParams(vmem_limit_bytes=VMEM_LIMIT)
    columns = proj_ab.reshape(channels, 2, 2, devices, part).transpose(2, 4, 3, 1, 0).reshape(2, 2 * hidden, channels)
    weight = jnp.pad(pair_mask.astype(jnp.float32).T, ((0, 0), (0, padded - rows)))
    normed, operands = pl.pallas_call(
        operands_kernel,
        out_shape=(
            jax.ShapeDtypeStruct((rows, cols, channels), jnp.bfloat16),
            jax.ShapeDtypeStruct((2 * hidden, cols, padded), jnp.bfloat16),
        ),
        in_specs=[VMEM] * 5,
        out_specs=(VMEM, VMEM),
        compiler_params=plain,
        name="operands",
    )(pair, weight, ln_in_gain.reshape(1, 1, channels), columns[0], columns[1])
    tri = pl.pallas_call(
        functools.partial(exchange_kernel, n_row, n_col, rows),
        out_shape=jax.ShapeDtypeStruct((part, devices, cols, padded), jnp.bfloat16),
        in_specs=[ANY],
        out_specs=ANY,
        scratch_shapes=[
            pltpu.VMEM((part, devices, 2, cols, padded), jnp.bfloat16),
            pltpu.VMEM((part, devices, cols, padded), jnp.bfloat16),
        ]
        + [pltpu.SemaphoreType.DMA((part,))] * 5,
        compiler_params=pltpu.CompilerParams(collective_id=0, has_side_effects=True, vmem_limit_bytes=VMEM_LIMIT),
        name="exchange",
    )(operands.reshape(part, devices, 2, cols, padded))
    gain = ln_out_gain.reshape(devices, part).T.reshape(hidden, 1, 1)
    mixing = out_weight.reshape(devices, part, channels).transpose(1, 0, 2).reshape(hidden, channels)
    return pl.pallas_call(
        update_kernel,
        out_shape=jax.ShapeDtypeStruct((rows, cols, channels), jnp.bfloat16),
        in_specs=[VMEM] * 5,
        out_specs=VMEM,
        compiler_params=plain,
        name="update",
    )(tri.reshape(hidden, cols, padded), normed, gain, gate_weight, mixing)


def solution(mesh):
    in_specs = (P("row", "col", None), P("row", "col"), P(), P(), P(), P(), P())
    out_specs = P("row", "col", None)
    return jax.shard_map(shards, mesh=mesh, in_specs=in_specs, out_specs=out_specs, check_vma=False)
```

```python
import functools

import jax
import jax.numpy as jnp
from jax import lax
from jax.experimental import pallas as pl
from jax.experimental.pallas import tpu as pltpu
from jax.sharding import PartitionSpec as P

EPS = 1e-05
LANES = 128
HALVES = 2
VMEM_LIMIT = 56 * 1024 * 1024
VMEM = pl.BlockSpec(memory_space=pltpu.VMEM)
ANY = pl.BlockSpec(memory_space=pl.ANY)


def chunks(length, size):
    return [(at, min(at + size, length)) for at in range(0, length, size)]


def pad_rows(values, to):
    short = to - values.shape[-2]
    if short == 0:
        return values
    shape = values.shape[:-2] + (short, values.shape[-1])
    return jnp.concatenate([values, jnp.zeros(shape, values.dtype)], axis=-2)


def layer_norm(values, gain, axis):
    middle = jnp.mean(values, axis=axis, keepdims=True)
    centred = values - middle
    spread = jnp.mean(centred * centred, axis=axis, keepdims=True)
    return centred * lax.rsqrt(spread + EPS) * gain


def operands_kernel(pair_ref, mask_ref, gain_ref, gates_ref, values_ref, normed_ref, out_ref):
    cols, padded = out_ref.shape[1], out_ref.shape[2]
    for low, high in chunks(cols, 8):
        normed = layer_norm(pair_ref[:, low:high, :].astype(jnp.float32), gain_ref[...], -1)
        normed_ref[:, low:high, :] = normed.astype(jnp.bfloat16)
        turned = pad_rows(jnp.transpose(normed, (1, 0, 2)), padded).astype(jnp.bfloat16)
        mine = []
        for at in range(high - low):
            turn = (((1,), (1,)), ((), ()))
            gates = lax.dot_general(gates_ref[...], turned[at], turn, preferred_element_type=jnp.float32)
            values = lax.dot_general(values_ref[...], turned[at], turn, preferred_element_type=jnp.float32)
            mine.append(jax.nn.sigmoid(gates) * values * mask_ref[low + at : low + at + 1, :])
        out_ref[:, low:high, :] = jnp.transpose(jnp.stack(mine), (1, 0, 2)).astype(jnp.bfloat16)


def exchange_kernel(
    n_row, n_col, rows, send_ref, out_ref, left, right, product,
    left_sent, left_came, right_sent, right_came, back_sent, back_came, own_left, own_right, own_back,
):
    steps, _, per, cols, padded = left.shape
    wide = n_col // HALVES
    owners = n_row * wide
    devices = n_row * n_col
    row, col = lax.axis_index("row"), lax.axis_index("col")
    half, spot = col // wide, lax.rem(col, wide)
    me, mine = row * n_col + col, row * wide + spot

    def anywhere(offset):
        other = lax.rem(me + offset, devices)
        to_row, to_col = other // n_col, lax.rem(other, n_col)
        return to_row * wide + lax.rem(to_col, wide), (to_row, to_col)

    def in_half(offset):
        other = lax.rem(mine + offset, owners)
        return other, (other // wide, half * wide + lax.rem(other, wide))

    barrier = pltpu.get_barrier_semaphore()

    def greet(offset, carry):
        pl.semaphore_signal(barrier, inc=1, device_id=anywhere(offset)[1], device_id_type=pl.DeviceIdType.MESH)
        return carry

    lax.fori_loop(1, devices, greet, 0)
    pl.semaphore_wait(barrier, devices - 1)

    def spread(count, place, source, target, sent, came):
        def one(offset, carry):
            other, device = place(offset)
            pltpu.make_async_remote_copy(
                src_ref=source.at[other],
                dst_ref=target,
                send_sem=sent,
                recv_sem=came,
                device_id=device,
                device_id_type=pl.DeviceIdType.MESH,
            ).start()
            return carry

        lax.fori_loop(1, count, one, 0)

    def own(h):
        return (
            pltpu.make_async_copy(send_ref.at[0, h, mine], left.at[h, me], own_left.at[h]),
            pltpu.make_async_copy(send_ref.at[1, h, mine], right.at[h, mine], own_right.at[h]),
        )

    def send(h, carry):
        for copy in own(h):
            copy.start()
        spread(devices, anywhere, send_ref.at[0, h], left.at[h, me], left_sent.at[h], left_came.at[h])
        spread(owners, in_half, send_ref.at[1, h], right.at[h, mine], right_sent.at[h], right_came.at[h])
        return carry

    lax.fori_loop(0, steps, send, 0)

    def wait_others(ref, count, sem):
        some = ref.at[pl.ds(0, count - 1)]
        pltpu.make_async_copy(some, some, sem).wait()

    def whole(held, h, p, width):
        pieces = [held[h, at * width : (at + 1) * width, p].reshape(width * cols, padded) for at in range(n_row)]
        return jnp.concatenate(pieces, axis=1)

    def own_result(h):
        return pltpu.make_async_copy(product.at[h, mine], out_ref.at[h, mine], own_back.at[h])

    def channels(h, carry):
        wait_others(left.at[h], devices, left_came.at[h])
        wait_others(right.at[h], owners, right_came.at[h])
        for copy in own(h):
            copy.wait()
        for p in range(per):
            firsts, seconds = whole(left, h, p, n_col), whole(right, h, p, wide)
            for at in range(n_row):
                panel = pad_rows(firsts[at * rows : (at + 1) * rows], padded)
                tri = lax.dot_general(seconds, panel, (((1,), (1,)), ((), ())), preferred_element_type=jnp.float32)
                product[h, at * wide : (at + 1) * wide, p] = tri.reshape(wide, cols, padded).astype(jnp.bfloat16)
        own_result(h).start()
        spread(owners, in_half, product.at[h], out_ref.at[h, mine], back_sent.at[h], back_came.at[h])
        return carry

    lax.fori_loop(0, steps, channels, 0)

    def finish(h, carry):
        wait_others(out_ref.at[h], owners, back_came.at[h])
        own_result(h).wait()
        wait_others(left.at[h], devices, left_sent.at[h])
        wait_others(right.at[h], owners, right_sent.at[h])
        wait_others(product.at[h], owners, back_sent.at[h])
        return carry

    lax.fori_loop(0, steps, finish, 0)


def update_kernel(tri_ref, normed_ref, gain_ref, gate_ref, weight_ref, out_ref):
    rows, cols, channels = normed_ref.shape
    for low, high in chunks(cols, 8):
        tri = layer_norm(tri_ref[:, low:high, :].astype(jnp.float32), gain_ref[...], 0)
        tri = jnp.transpose(tri, (1, 0, 2)).astype(jnp.bfloat16)
        mixed = []
        for at in range(high - low):
            turn = (((0,), (0,)), ((), ()))
            mixed.append(lax.dot_general(tri[at], weight_ref[...], turn, preferred_element_type=jnp.float32)[:rows])
        mixed = jnp.transpose(jnp.stack(mixed), (1, 0, 2))
        normed = normed_ref[:, low:high, :].astype(jnp.float32).reshape(rows * (high - low), channels)
        gate = jnp.dot(normed.astype(jnp.bfloat16), gate_ref[...], preferred_element_type=jnp.float32)
        gate = jax.nn.sigmoid(gate).reshape(rows, high - low, channels)
        out_ref[:, low:high, :] = (gate * mixed).astype(jnp.bfloat16)


def shards(pair, pair_mask, ln_in_gain, proj_ab, gate_weight, ln_out_gain, out_weight):
    rows, cols, channels = pair.shape
    hidden = out_weight.shape[0]
    n_row, n_col = lax.axis_size("row"), lax.axis_size("col")
    devices = n_row * n_col
    owners = devices // HALVES
    part = hidden // owners
    per = min(part, 2)
    steps = part // per
    padded = -(-rows // LANES) * LANES
    plain = pltpu.CompilerParams(vmem_limit_bytes=VMEM_LIMIT)
    columns = proj_ab.reshape(channels, 2, 2, owners, steps, per).transpose(2, 1, 4, 3, 5, 0)
    columns = columns.reshape(2, 2 * hidden, channels)
    weight = jnp.pad(pair_mask.astype(jnp.float32).T, ((0, 0), (0, padded - rows)))
    normed, operands = pl.pallas_call(
        operands_kernel,
        out_shape=(
            jax.ShapeDtypeStruct((rows, cols, channels), jnp.bfloat16),
            jax.ShapeDtypeStruct((2 * hidden, cols, padded), jnp.bfloat16),
        ),
        in_specs=[VMEM] * 5,
        out_specs=(VMEM, VMEM),
        compiler_params=plain,
        name="operands",
    )(pair, weight, ln_in_gain.reshape(1, 1, channels), columns[0], columns[1])
    tri = pl.pallas_call(
        functools.partial(exchange_kernel, n_row, n_col, rows),
        out_shape=jax.ShapeDtypeStruct((steps, owners, per, cols, padded), jnp.bfloat16),
        in_specs=[ANY],
        out_specs=ANY,
        scratch_shapes=[
            pltpu.VMEM((steps, devices, per, cols, padded), jnp.bfloat16),
            pltpu.VMEM((steps, owners, per, cols, padded), jnp.bfloat16),
            pltpu.VMEM((steps, owners, per, cols, padded), jnp.bfloat16),
        ]
        + [pltpu.SemaphoreType.DMA((steps,))] * 9,
        compiler_params=pltpu.CompilerParams(collective_id=0, has_side_effects=True, vmem_limit_bytes=VMEM_LIMIT),
        name="exchange",
    )(operands.reshape(2, steps, owners, per, cols, padded))
    gain = ln_out_gain.reshape(owners, steps, per).transpose(1, 0, 2).reshape(hidden, 1, 1)
    mixing = out_weight.reshape(owners, steps, per, channels).transpose(1, 0, 2, 3).reshape(hidden, channels)
    return pl.pallas_call(
        update_kernel,
        out_shape=jax.ShapeDtypeStruct((rows, cols, channels), jnp.bfloat16),
        in_specs=[VMEM] * 5,
        out_specs=VMEM,
        compiler_params=plain,
        name="update",
    )(tri.reshape(hidden, cols, padded), normed, gain, gate_weight, mixing)


def solution(mesh):
    in_specs = (P("row", "col", None), P("row", "col"), P(), P(), P(), P(), P())
    out_specs = P("row", "col", None)
    return jax.shard_map(shards, mesh=mesh, in_specs=in_specs, out_specs=out_specs, check_vma=False)
```

```python
import functools

import jax
import jax.numpy as jnp
from jax import lax
from jax.experimental import pallas as pl
from jax.experimental.pallas import tpu as pltpu
from jax.sharding import PartitionSpec as P

EPS = 1e-05
LANES = 128
VMEM_LIMIT = 56 * 1024 * 1024
VMEM = pl.BlockSpec(memory_space=pltpu.VMEM)
ANY = pl.BlockSpec(memory_space=pl.ANY)


def chunks(length, size):
    return [(at, min(at + size, length)) for at in range(0, length, size)]


def pad_rows(values, to):
    short = to - values.shape[-2]
    if short == 0:
        return values
    shape = values.shape[:-2] + (short, values.shape[-1])
    return jnp.concatenate([values, jnp.zeros(shape, values.dtype)], axis=-2)


def layer_norm(values, gain, axis):
    middle = jnp.mean(values, axis=axis, keepdims=True)
    centred = values - middle
    spread = jnp.mean(centred * centred, axis=axis, keepdims=True)
    return centred * lax.rsqrt(spread + EPS) * gain


def operands_kernel(pair_ref, mask_ref, gain_ref, gates_ref, values_ref, normed_ref, out_ref):
    cols, padded = out_ref.shape[1], out_ref.shape[2]
    for low, high in chunks(cols, 8):
        normed = layer_norm(pair_ref[:, low:high, :].astype(jnp.float32), gain_ref[...], -1)
        normed_ref[:, low:high, :] = normed.astype(jnp.bfloat16)
        turned = pad_rows(jnp.transpose(normed, (1, 0, 2)), padded).astype(jnp.bfloat16)
        mine = []
        for at in range(high - low):
            turn = (((1,), (1,)), ((), ()))
            gates = lax.dot_general(gates_ref[...], turned[at], turn, preferred_element_type=jnp.float32)
            values = lax.dot_general(values_ref[...], turned[at], turn, preferred_element_type=jnp.float32)
            mine.append(jax.nn.sigmoid(gates) * values * mask_ref[low + at : low + at + 1, :])
        out_ref[:, low:high, :] = jnp.transpose(jnp.stack(mine), (1, 0, 2)).astype(jnp.bfloat16)


def exchange_kernel(
    n_row, n_col, rows, ends, send_ref, out_ref, left, right, product,
    left_sent, left_came, far_sent, far_came, relay_sent, right_sent, right_came, back_sent, back_came,
):
    steps, _, fellows, per, cols, padded = left.shape
    wide, quarter = n_col // 2, n_col // 4
    owners = n_row * quarter
    devices = n_row * n_col
    row, col = lax.axis_index("row"), lax.axis_index("col")
    half, spot = col // wide, lax.rem(col, wide)
    place, seat = spot // quarter, lax.rem(spot, quarter)
    middle = lax.rem(place + half, 2)
    mine, me = row * wide + spot, row * quarter + seat

    def owner_at(other, in_half, to_middle):
        shift = lax.rem(in_half + to_middle, 2) * quarter
        return other // quarter, in_half * wide + shift + lax.rem(other, quarter)

    barrier = pltpu.get_barrier_semaphore()

    def greet(offset, carry):
        other = lax.rem(row * n_col + col + offset, devices)
        device = other // n_col, lax.rem(other, n_col)
        pl.semaphore_signal(barrier, inc=1, device_id=device, device_id_type=pl.DeviceIdType.MESH)
        return carry

    lax.fori_loop(1, devices, greet, 0)
    pl.semaphore_wait(barrier, devices - 1)

    def remote(source, target, sent, came, device):
        return pltpu.make_async_remote_copy(
            src_ref=source,
            dst_ref=target,
            send_sem=sent,
            recv_sem=came,
            device_id=device,
            device_id_type=pl.DeviceIdType.MESH,
        )

    def to_owners(source, target, sent, came, in_half, to_middle, skip):
        def one(offset, carry):
            other = lax.rem(me + offset, owners)
            remote(source.at[other], target, sent, came, owner_at(other, in_half, to_middle)).start()
            return carry

        lax.fori_loop(skip, owners, one, 0)

    def belongs(h):
        return middle if h >= ends else 1 - middle

    def send(side, h):
        target, sent, came = (left.at[h, half], left_sent, left_came) if side == 0 else (right.at[h], right_sent, right_came)
        member = belongs(h)

        @pl.when(member == 1)
        def _():
            pltpu.make_async_copy(send_ref.at[side, h, me], target.at[mine], came.at[h]).start()

        to_owners(send_ref.at[side, h], target.at[mine], sent.at[h], came.at[h], half, int(h >= ends), member)

    def send_far(h):
        to_owners(send_ref.at[0, h], left.at[h, half, mine], far_sent.at[h], far_came.at[h], 1 - half, 0, 0)

    send(0, ends)
    for h in range(ends):
        send_far(h)
        send(0, h)
        send(1, h)
    for h in range(ends, steps):
        if h > ends:
            send(0, h)
        send(1, h)

    def wait_for(ref, sem):
        pltpu.make_async_copy(ref, ref, sem).wait()

    def relay(h):
        return remote(
            left.at[h, half], left.at[h, half], relay_sent.at[h], far_came.at[h], (row, owner_at(me, 1 - half, 1)[1])
        )

    def pass_on(h):
        wait_for(left.at[h, half], left_came.at[h])
        relay(h).start()

    def channels(h):
        wait_for(right.at[h], right_came.at[h])
        wait_for(left.at[h, 1 - half], far_came.at[h])
        for p in range(per):
            firsts, seconds = [], []
            for at in range(n_row):
                span = slice(at * wide, (at + 1) * wide)
                both = [left[h, side, span, p].reshape(wide * cols, padded) for side in range(2)]
                firsts.append(jnp.concatenate(both, axis=0))
                seconds.append(right[h, span, p].reshape(wide * cols, padded))
            firsts, seconds = jnp.concatenate(firsts, axis=1), jnp.concatenate(seconds, axis=1)
            for at in range(n_row):
                panel = pad_rows(firsts[at * rows : (at + 1) * rows], padded)
                tri = lax.dot_general(seconds, panel, (((1,), (1,)), ((), ())), preferred_element_type=jnp.float32)
                product[h, at * wide : (at + 1) * wide, p] = tri.reshape(wide, cols, padded).astype(jnp.bfloat16)
        pltpu.make_async_copy(product.at[h, mine], out_ref.at[h, me], back_came.at[h]).start()

        def one(offset, carry):
            other = lax.rem(mine + offset, fellows)
            device = other // wide, half * wide + lax.rem(other, wide)
            remote(product.at[h, other], out_ref.at[h, me], back_sent.at[h], back_came.at[h], device).start()
            return carry

        lax.fori_loop(1, fellows, one, 0)

    ahead = min(3, steps - ends)

    @pl.when(middle == 1)
    def _():
        for h in range(ends, ends + ahead):
            pass_on(h)

        def one(h, carry):
            pass_on(h + ahead)
            channels(h)
            return carry

        def last(h, carry):
            channels(h)
            return carry

        lax.fori_loop(ends, steps - ahead, one, 0)
        lax.fori_loop(steps - ahead, steps, last, 0)

    @pl.when(middle == 0)
    def _():
        def one(h, carry):
            wait_for(left.at[h, half], left_came.at[h])
            channels(h)
            return carry

        lax.fori_loop(0, ends, one, 0)

    for h in range(steps):
        member = belongs(h)
        wait_for(out_ref.at[h], back_came.at[h])
        if h < ends:
            wait_for(left.at[h, 0, pl.ds(0, owners)], far_sent.at[h])

        @pl.when(member == 1)
        def _():
            others = left.at[h, 0, pl.ds(0, owners - 1)]
            wait_for(others, left_sent.at[h])
            wait_for(others, right_sent.at[h])
            wait_for(product.at[h, pl.ds(0, fellows - 1)], back_sent.at[h])
            if h >= ends:
                wait_for(left.at[h, half], relay_sent.at[h])

        @pl.when(member == 0)
        def _():
            everyone = left.at[h, 0, pl.ds(0, owners)]
            wait_for(everyone, left_sent.at[h])
            wait_for(everyone, right_sent.at[h])


def update_kernel(tri_ref, normed_ref, gain_ref, gate_ref, weight_ref, out_ref):
    rows, cols, channels = normed_ref.shape
    for low, high in chunks(cols, 8):
        tri = layer_norm(tri_ref[:, low:high, :].astype(jnp.float32), gain_ref[...], 0)
        tri = jnp.transpose(tri, (1, 0, 2)).astype(jnp.bfloat16)
        mixed = []
        for at in range(high - low):
            turn = (((0,), (0,)), ((), ()))
            mixed.append(lax.dot_general(tri[at], weight_ref[...], turn, preferred_element_type=jnp.float32)[:rows])
        mixed = jnp.transpose(jnp.stack(mixed), (1, 0, 2))
        normed = normed_ref[:, low:high, :].astype(jnp.float32).reshape(rows * (high - low), channels)
        gate = jnp.dot(normed.astype(jnp.bfloat16), gate_ref[...], preferred_element_type=jnp.float32)
        gate = jax.nn.sigmoid(gate).reshape(rows, high - low, channels)
        out_ref[:, low:high, :] = (gate * mixed).astype(jnp.bfloat16)


def shards(pair, pair_mask, ln_in_gain, proj_ab, gate_weight, ln_out_gain, out_weight):
    rows, cols, channels = pair.shape
    hidden = out_weight.shape[0]
    n_row, n_col = lax.axis_size("row"), lax.axis_size("col")
    fellows = n_row * (n_col // 2)
    owners = n_row * (n_col // 4)
    part = hidden // owners
    per = max(part // 8, 1)
    steps = part // per
    ends = steps // 4
    padded = -(-rows // LANES) * LANES
    plain = pltpu.CompilerParams(vmem_limit_bytes=VMEM_LIMIT)
    columns = proj_ab.reshape(channels, 2, 2, owners, steps, per).transpose(2, 1, 4, 3, 5, 0)
    columns = columns.reshape(2, 2 * hidden, channels)
    weight = jnp.pad(pair_mask.astype(jnp.float32).T, ((0, 0), (0, padded - rows)))
    normed, operands = pl.pallas_call(
        operands_kernel,
        out_shape=(
            jax.ShapeDtypeStruct((rows, cols, channels), jnp.bfloat16),
            jax.ShapeDtypeStruct((2 * hidden, cols, padded), jnp.bfloat16),
        ),
        in_specs=[VMEM] * 5,
        out_specs=(VMEM, VMEM),
        compiler_params=plain,
        name="operands",
    )(pair, weight, ln_in_gain.reshape(1, 1, channels), columns[0], columns[1])
    tri = pl.pallas_call(
        functools.partial(exchange_kernel, n_row, n_col, rows, ends),
        out_shape=jax.ShapeDtypeStruct((steps, owners, per, cols, padded), jnp.bfloat16),
        in_specs=[ANY],
        out_specs=ANY,
        scratch_shapes=[
            pltpu.VMEM((steps, 2, fellows, per, cols, padded), jnp.bfloat16),
            pltpu.VMEM((steps, fellows, per, cols, padded), jnp.bfloat16),
            pltpu.VMEM((steps, fellows, per, cols, padded), jnp.bfloat16),
        ]
        + [pltpu.SemaphoreType.DMA((steps,))] * 9,
        compiler_params=pltpu.CompilerParams(collective_id=0, has_side_effects=True, vmem_limit_bytes=VMEM_LIMIT),
        name="exchange",
    )(operands.reshape(2, steps, owners, per, cols, padded))
    gain = ln_out_gain.reshape(owners, steps, per).transpose(1, 0, 2).reshape(hidden, 1, 1)
    mixing = out_weight.reshape(owners, steps, per, channels).transpose(1, 0, 2, 3).reshape(hidden, channels)
    return pl.pallas_call(
        update_kernel,
        out_shape=jax.ShapeDtypeStruct((rows, cols, channels), jnp.bfloat16),
        in_specs=[VMEM] * 5,
        out_specs=VMEM,
        compiler_params=plain,
        name="update",
    )(tri.reshape(hidden, cols, padded), normed, gain, gate_weight, mixing)


def solution(mesh):
    in_specs = (P("row", "col", None), P("row", "col"), P(), P(), P(), P(), P())
    out_specs = P("row", "col", None)
    return jax.shard_map(shards, mesh=mesh, in_specs=in_specs, out_specs=out_specs, check_vma=False)
```

```python
import functools

import jax
import jax.numpy as jnp
from jax import lax
from jax.experimental import pallas as pl
from jax.experimental.pallas import tpu as pltpu
from jax.sharding import PartitionSpec as P

EPS = 1e-05
LANES = 128
VMEM_LIMIT = 56 * 1024 * 1024
VMEM = pl.BlockSpec(memory_space=pltpu.VMEM)


def chunks(length, size):
    return [(at, min(at + size, length)) for at in range(0, length, size)]


def pad_rows(values, to):
    short = to - values.shape[-2]
    if short == 0:
        return values
    shape = values.shape[:-2] + (short, values.shape[-1])
    return jnp.concatenate([values, jnp.zeros(shape, values.dtype)], axis=-2)


def layer_norm(values, gain, axis):
    middle = jnp.mean(values, axis=axis, keepdims=True)
    centred = values - middle
    spread = jnp.mean(centred * centred, axis=axis, keepdims=True)
    return centred * lax.rsqrt(spread + EPS) * gain


def triangle_kernel(
    n_row, n_col, ends, pair_ref, mask_ref, in_gain_ref, proj_ref, gate_ref, out_gain_ref, weight_ref, update_ref,
    turned, gates, operands, left, right, product, landed, left_sent, left_came, far_sent, far_came, relay_sent, right_sent, right_came, back_sent, back_came,
):
    steps, _, fellows, per, cols, padded = left.shape
    rows, channels = pair_ref.shape[0], pair_ref.shape[2]
    hidden = weight_ref.shape[0]
    wide, quarter = n_col // 2, n_col // 4
    owners = n_row * quarter
    devices = n_row * n_col
    row, col = lax.axis_index("row"), lax.axis_index("col")
    half, spot = col // wide, lax.rem(col, wide)
    place, seat = spot // quarter, lax.rem(spot, quarter)
    middle = lax.rem(place + half, 2)
    mine, me = row * wide + spot, row * quarter + seat

    def owner_at(other, in_half, to_middle):
        shift = lax.rem(in_half + to_middle, 2) * quarter
        return other // quarter, in_half * wide + shift + lax.rem(other, quarter)

    barrier = pltpu.get_barrier_semaphore()

    def greet(offset, carry):
        other = lax.rem(row * n_col + col + offset, devices)
        device = other // n_col, lax.rem(other, n_col)
        pl.semaphore_signal(barrier, inc=1, device_id=device, device_id_type=pl.DeviceIdType.MESH)
        return carry

    lax.fori_loop(1, devices, greet, 0)

    for low, high in chunks(cols, 8):
        normed = layer_norm(pair_ref[:, low:high, :].astype(jnp.float32), in_gain_ref[...], -1)
        turned[low:high] = pad_rows(jnp.transpose(normed, (1, 0, 2)), padded).astype(jnp.bfloat16)

    def make(side):
        weights = jnp.transpose(proj_ref[:, side * 2 * hidden : (side + 1) * 2 * hidden].astype(jnp.float32))
        weights = weights.astype(jnp.bfloat16)
        for low, high in chunks(cols, 8):
            rest = jnp.zeros((high - low, padded - rows), jnp.float32)
            valid = jnp.concatenate([mask_ref[low:high, :].astype(jnp.float32), rest], axis=1)
            each = []
            for at in range(low, high):
                projected = lax.dot_general(
                    weights, turned[at], (((1,), (1,)), ((), ())), preferred_element_type=jnp.float32
                )
                each.append(jax.nn.sigmoid(projected[:hidden]) * projected[hidden:] * valid[at - low : at - low + 1])
            each = jnp.transpose(jnp.stack(each), (1, 0, 2)).astype(jnp.bfloat16)
            operands[side, :, :, :, low:high, :] = each.reshape(owners, steps, per, high - low, padded)

    make(0)
    pl.semaphore_wait(barrier, devices - 1)

    def remote(source, target, sent, came, device):
        return pltpu.make_async_remote_copy(
            src_ref=source,
            dst_ref=target,
            send_sem=sent,
            recv_sem=came,
            device_id=device,
            device_id_type=pl.DeviceIdType.MESH,
        )

    def to_owners(source, target, sent, came, in_half, to_middle, skip):
        def one(offset, carry):
            other = lax.rem(me + offset, owners)
            remote(source(other), target, sent, came, owner_at(other, in_half, to_middle)).start()
            return carry

        lax.fori_loop(skip, owners, one, 0)

    def belongs(h):
        return middle if h >= ends else 1 - middle

    def send(side, h):
        target, sent, came = (left.at[h, half], left_sent, left_came) if side == 0 else (right.at[h], right_sent, right_came)
        member = belongs(h)

        @pl.when(member == 1)
        def _():
            pltpu.make_async_copy(operands.at[side, me, h], target.at[mine], came.at[h]).start()

        to_owners(lambda other: operands.at[side, other, h], target.at[mine], sent.at[h], came.at[h], half, int(h >= ends), member)

    def send_far(h):
        target = left.at[h, half, mine]
        to_owners(lambda other: operands.at[0, other, h], target, far_sent.at[h], far_came.at[h], 1 - half, 0, 0)

    send(0, ends)
    for h in range(ends):
        send_far(h)
        send(0, h)
    for h in range(ends + 1, steps):
        send(0, h)
    make(1)
    for h in range(steps):
        send(1, h)

    def open_gate(at, carry):
        gate = jnp.dot(turned[at], gate_ref[...], preferred_element_type=jnp.float32)
        gates[at] = jax.nn.sigmoid(gate)
        return carry

    lax.fori_loop(0, cols, open_gate, 0)

    def wait_for(ref, sem):
        pltpu.make_async_copy(ref, ref, sem).wait()

    def relay(h):
        return remote(
            left.at[h, half], left.at[h, half], relay_sent.at[h], far_came.at[h], (row, owner_at(me, 1 - half, 1)[1])
        )

    def pass_on(h):
        wait_for(left.at[h, half], left_came.at[h])
        relay(h).start()

    def channels(h):
        wait_for(right.at[h], right_came.at[h])
        wait_for(left.at[h, 1 - half], far_came.at[h])
        for p in range(per):
            firsts, seconds = [], []
            for at in range(n_row):
                span = slice(at * wide, (at + 1) * wide)
                both = [left[h, side, span, p].reshape(wide * cols, padded) for side in range(2)]
                firsts.append(jnp.concatenate(both, axis=0))
                seconds.append(right[h, span, p].reshape(wide * cols, padded))
            firsts, seconds = jnp.concatenate(firsts, axis=1), jnp.concatenate(seconds, axis=1)
            for at in range(n_row):
                panel = pad_rows(firsts[at * rows : (at + 1) * rows], padded)
                tri = lax.dot_general(seconds, panel, (((1,), (1,)), ((), ())), preferred_element_type=jnp.float32)
                product[h, at * wide : (at + 1) * wide, p] = tri.reshape(wide, cols, padded).astype(jnp.bfloat16)
        pltpu.make_async_copy(product.at[h, mine], landed.at[me, h], back_came.at[h]).start()

        def one(offset, carry):
            other = lax.rem(mine + offset, fellows)
            device = other // wide, half * wide + lax.rem(other, wide)
            remote(product.at[h, other], landed.at[me, h], back_sent.at[h], back_came.at[h], device).start()
            return carry

        lax.fori_loop(1, fellows, one, 0)

    ahead = min(3, steps - ends)

    @pl.when(middle == 1)
    def _():
        for h in range(ends, ends + ahead):
            pass_on(h)

        def one(h, carry):
            pass_on(h + ahead)
            channels(h)
            return carry

        def last(h, carry):
            channels(h)
            return carry

        lax.fori_loop(ends, steps - ahead, one, 0)
        lax.fori_loop(steps - ahead, steps, last, 0)

    @pl.when(middle == 0)
    def _():
        def one(h, carry):
            wait_for(left.at[h, half], left_came.at[h])
            channels(h)
            return carry

        lax.fori_loop(0, ends, one, 0)

    for h in range(steps):
        member = belongs(h)
        wait_for(landed.at[:, h], back_came.at[h])
        if h < ends:
            wait_for(left.at[h, 0, pl.ds(0, owners)], far_sent.at[h])

        @pl.when(member == 1)
        def _():
            others = left.at[h, 0, pl.ds(0, owners - 1)]
            wait_for(others, left_sent.at[h])
            wait_for(others, right_sent.at[h])
            wait_for(product.at[h, pl.ds(0, fellows - 1)], back_sent.at[h])
            if h >= ends:
                wait_for(left.at[h, half], relay_sent.at[h])

        @pl.when(member == 0)
        def _():
            everyone = left.at[h, 0, pl.ds(0, owners)]
            wait_for(everyone, left_sent.at[h])
            wait_for(everyone, right_sent.at[h])

    for low, high in chunks(cols, 8):
        tri = landed[:, :, :, low:high, :].astype(jnp.float32).reshape(hidden, high - low, padded)
        tri = jnp.transpose(layer_norm(tri, out_gain_ref[...], 0), (1, 0, 2)).astype(jnp.bfloat16)
        mixed = []
        for at in range(low, high):
            mix = lax.dot_general(
                tri[at - low], weight_ref[...], (((0,), (0,)), ((), ())), preferred_element_type=jnp.float32
            )
            mixed.append((gates[at] * mix)[:rows])
        update_ref[:, low:high, :] = jnp.transpose(jnp.stack(mixed), (1, 0, 2)).astype(jnp.bfloat16)


def shards(pair, pair_mask, ln_in_gain, proj_ab, gate_weight, ln_out_gain, out_weight):
    rows, cols, channels = pair.shape
    hidden = out_weight.shape[0]
    n_row, n_col = lax.axis_size("row"), lax.axis_size("col")
    fellows = n_row * (n_col // 2)
    owners = n_row * (n_col // 4)
    part = hidden // owners
    per = max(part // 8, 1)
    steps = part // per
    ends = steps // 4
    padded = -(-rows // LANES) * LANES
    block = (per, cols, padded)
    return pl.pallas_call(
        functools.partial(triangle_kernel, n_row, n_col, ends),
        out_shape=jax.ShapeDtypeStruct((rows, cols, channels), jnp.bfloat16),
        in_specs=[VMEM] * 7,
        out_specs=VMEM,
        scratch_shapes=[
            pltpu.VMEM((cols, padded, channels), jnp.bfloat16),
            pltpu.VMEM((cols, padded, channels), jnp.float32),
            pltpu.VMEM((2, owners, steps) + block, jnp.bfloat16),
            pltpu.VMEM((steps, 2, fellows) + block, jnp.bfloat16),
            pltpu.VMEM((steps, fellows) + block, jnp.bfloat16),
            pltpu.VMEM((steps, fellows) + block, jnp.bfloat16),
            pltpu.VMEM((owners, steps) + block, jnp.bfloat16),
        ]
        + [pltpu.SemaphoreType.DMA((steps,))] * 9,
        compiler_params=pltpu.CompilerParams(collective_id=0, has_side_effects=True, vmem_limit_bytes=VMEM_LIMIT),
        name="triangle",
    )(
        pair,
        pair_mask.T,
        ln_in_gain.reshape(1, 1, channels),
        proj_ab,
        gate_weight,
        ln_out_gain.reshape(hidden, 1, 1),
        out_weight,
    )


def solution(mesh):
    in_specs = (P("row", "col", None), P("row", "col"), P(), P(), P(), P(), P())
    out_specs = P("row", "col", None)
    return jax.shard_map(shards, mesh=mesh, in_specs=in_specs, out_specs=out_specs, check_vma=False)
```

```python
import functools

import jax
import jax.numpy as jnp
from jax import lax
from jax.experimental import pallas as pl
from jax.experimental.pallas import tpu as pltpu
from jax.sharding import PartitionSpec as P

EPS = 1e-05
LANES = 128
VMEM_LIMIT = 56 * 1024 * 1024
VMEM = pl.BlockSpec(memory_space=pltpu.VMEM)


def chunks(length, size):
    return [(at, min(at + size, length)) for at in range(0, length, size)]


def pad_rows(values, to):
    short = to - values.shape[-2]
    if short == 0:
        return values
    shape = values.shape[:-2] + (short, values.shape[-1])
    return jnp.concatenate([values, jnp.zeros(shape, values.dtype)], axis=-2)


def layer_norm(values, axis):
    middle = jnp.mean(values, axis=axis, keepdims=True)
    centred = values - middle
    spread = jnp.mean(centred * centred, axis=axis, keepdims=True)
    return centred * lax.rsqrt(spread + EPS)


def triangle_kernel(
    n_row, n_col, ends, pair_ref, mask_ref, in_gain_ref, proj_ref, gate_ref, out_gain_ref, weight_ref, update_ref,
    turned, gates, operands, left, right, product, landed, left_sent, left_came, far_sent, far_came, relay_sent, right_sent, right_came, back_sent, back_came,
):
    steps, _, fellows, per, cols, padded = left.shape
    rows, channels = pair_ref.shape[0], pair_ref.shape[2]
    hidden = weight_ref.shape[0]
    wide, quarter = n_col // 2, n_col // 4
    owners = n_row * quarter
    devices = n_row * n_col
    row, col = lax.axis_index("row"), lax.axis_index("col")
    half, spot = col // wide, lax.rem(col, wide)
    place, seat = spot // quarter, lax.rem(spot, quarter)
    middle = lax.rem(place + half, 2)
    mine, me = row * wide + spot, row * quarter + seat

    def owner_at(other, in_half, to_middle):
        shift = lax.rem(in_half + to_middle, 2) * quarter
        return other // quarter, in_half * wide + shift + lax.rem(other, quarter)

    barrier = pltpu.get_barrier_semaphore()

    def greet(offset, carry):
        other = lax.rem(row * n_col + col + offset, devices)
        device = other // n_col, lax.rem(other, n_col)
        pl.semaphore_signal(barrier, inc=1, device_id=device, device_id_type=pl.DeviceIdType.MESH)
        return carry

    lax.fori_loop(1, devices, greet, 0)

    for low, high in chunks(cols, 8):
        normed = layer_norm(pair_ref[:, low:high, :].astype(jnp.float32), -1) * in_gain_ref[...]
        turned[low:high] = pad_rows(jnp.transpose(normed, (1, 0, 2)), padded).astype(jnp.bfloat16)

    def make(side):
        weights = jnp.transpose(proj_ref[:, side * 2 * hidden : (side + 1) * 2 * hidden].astype(jnp.float32))
        weights = weights.astype(jnp.bfloat16)
        for low, high in chunks(cols, 8):
            rest = jnp.zeros((high - low, padded - rows), jnp.float32)
            valid = jnp.concatenate([mask_ref[low:high, :].astype(jnp.float32), rest], axis=1)
            each = []
            for at in range(low, high):
                projected = lax.dot_general(
                    weights, turned[at], (((1,), (1,)), ((), ())), preferred_element_type=jnp.float32
                )
                each.append(jax.nn.sigmoid(projected[:hidden]) * projected[hidden:] * valid[at - low : at - low + 1])
            each = jnp.transpose(jnp.stack(each), (1, 0, 2)).astype(jnp.bfloat16)
            operands[side, :, :, :, low:high, :] = each.reshape(owners, steps, per, high - low, padded)

    make(0)
    pl.semaphore_wait(barrier, devices - 1)

    def remote(source, target, sent, came, device):
        return pltpu.make_async_remote_copy(
            src_ref=source,
            dst_ref=target,
            send_sem=sent,
            recv_sem=came,
            device_id=device,
            device_id_type=pl.DeviceIdType.MESH,
        )

    def to_owners(source, target, sent, came, in_half, to_middle, skip):
        def one(offset, carry):
            other = lax.rem(me + offset, owners)
            remote(source(other), target, sent, came, owner_at(other, in_half, to_middle)).start()
            return carry

        lax.fori_loop(skip, owners, one, 0)

    def belongs(h):
        return middle if h >= ends else 1 - middle

    def send(side, h):
        target, sent, came = (left.at[h, half], left_sent, left_came) if side == 0 else (right.at[h], right_sent, right_came)
        member = belongs(h)

        @pl.when(member == 1)
        def _():
            pltpu.make_async_copy(operands.at[side, me, h], target.at[mine], came.at[h]).start()

        to_owners(lambda other: operands.at[side, other, h], target.at[mine], sent.at[h], came.at[h], half, int(h >= ends), member)

    def send_far(h):
        target = left.at[h, half, mine]
        to_owners(lambda other: operands.at[0, other, h], target, far_sent.at[h], far_came.at[h], 1 - half, 0, 0)

    send(0, ends)
    for h in range(ends):
        send_far(h)
        send(0, h)
    for h in range(ends + 1, steps):
        send(0, h)
    make(1)
    for h in range(steps):
        send(1, h)

    def open_gate(at, carry):
        gate = jnp.dot(turned[at], gate_ref[...], preferred_element_type=jnp.float32)
        gates[at] = jax.nn.sigmoid(gate)
        return carry

    lax.fori_loop(0, cols, open_gate, 0)

    def wait_for(ref, sem):
        pltpu.make_async_copy(ref, ref, sem).wait()

    def relay(h):
        return remote(
            left.at[h, half], left.at[h, half], relay_sent.at[h], far_came.at[h], (row, owner_at(me, 1 - half, 1)[1])
        )

    def pass_on(h):
        wait_for(left.at[h, half], left_came.at[h])
        relay(h).start()

    def channels(h):
        wait_for(right.at[h], right_came.at[h])
        wait_for(left.at[h, 1 - half], far_came.at[h])
        for p in range(per):
            firsts, seconds = [], []
            for at in range(n_row):
                span = slice(at * wide, (at + 1) * wide)
                both = [left[h, side, span, p].reshape(wide * cols, padded) for side in range(2)]
                firsts.append(jnp.concatenate(both, axis=0))
                seconds.append(right[h, span, p].reshape(wide * cols, padded))
            firsts, seconds = jnp.concatenate(firsts, axis=1), jnp.concatenate(seconds, axis=1)
            for at in range(n_row):
                panel = pad_rows(firsts[at * rows : (at + 1) * rows], padded)
                tri = lax.dot_general(seconds, panel, (((1,), (1,)), ((), ())), preferred_element_type=jnp.float32)
                product[h, at * wide : (at + 1) * wide, p] = tri.reshape(wide, cols, padded).astype(jnp.bfloat16)
        pltpu.make_async_copy(product.at[h, mine], landed.at[me, h], back_came.at[h]).start()

        def one(offset, carry):
            other = lax.rem(mine + offset, fellows)
            device = other // wide, half * wide + lax.rem(other, wide)
            remote(product.at[h, other], landed.at[me, h], back_sent.at[h], back_came.at[h], device).start()
            return carry

        lax.fori_loop(1, fellows, one, 0)

    ahead = steps - ends

    @pl.when(middle == 1)
    def _():
        for h in range(ends, ends + ahead):
            pass_on(h)

        def one(h, carry):
            pass_on(h + ahead)
            channels(h)
            return carry

        def last(h, carry):
            channels(h)
            return carry

        lax.fori_loop(ends, steps - ahead, one, 0)
        lax.fori_loop(steps - ahead, steps, last, 0)

    @pl.when(middle == 0)
    def _():
        def one(h, carry):
            wait_for(left.at[h, half], left_came.at[h])
            channels(h)
            return carry

        lax.fori_loop(0, ends, one, 0)

    for h in range(steps):
        member = belongs(h)
        wait_for(landed.at[:, h], back_came.at[h])
        if h < ends:
            wait_for(left.at[h, 0, pl.ds(0, owners)], far_sent.at[h])

        @pl.when(member == 1)
        def _():
            others = left.at[h, 0, pl.ds(0, owners - 1)]
            wait_for(others, left_sent.at[h])
            wait_for(others, right_sent.at[h])
            wait_for(product.at[h, pl.ds(0, fellows - 1)], back_sent.at[h])
            if h >= ends:
                wait_for(left.at[h, half], relay_sent.at[h])

        @pl.when(member == 0)
        def _():
            everyone = left.at[h, 0, pl.ds(0, owners)]
            wait_for(everyone, left_sent.at[h])
            wait_for(everyone, right_sent.at[h])

    out_gain = jnp.transpose(jnp.broadcast_to(out_gain_ref[...], (padded, hidden)))
    for low, high in chunks(cols, 8):
        tri = landed[:, :, :, low:high, :].astype(jnp.float32).reshape(hidden, high - low, padded)
        tri = (jnp.transpose(layer_norm(tri, 0), (1, 0, 2)) * out_gain).astype(jnp.bfloat16)
        mixed = []
        for at in range(low, high):
            mix = lax.dot_general(
                tri[at - low], weight_ref[...], (((0,), (0,)), ((), ())), preferred_element_type=jnp.float32
            )
            mixed.append((gates[at] * mix)[:rows])
        update_ref[:, low:high, :] = jnp.transpose(jnp.stack(mixed), (1, 0, 2)).astype(jnp.bfloat16)


def shards(pair, pair_mask, ln_in_gain, proj_ab, gate_weight, ln_out_gain, out_weight):
    rows, cols, channels = pair.shape
    hidden = out_weight.shape[0]
    n_row, n_col = lax.axis_size("row"), lax.axis_size("col")
    fellows = n_row * (n_col // 2)
    owners = n_row * (n_col // 4)
    part = hidden // owners
    per = max(part // 16, 1)
    steps = part // per
    ends = steps // 4
    padded = -(-rows // LANES) * LANES
    block = (per, cols, padded)
    return pl.pallas_call(
        functools.partial(triangle_kernel, n_row, n_col, ends),
        out_shape=jax.ShapeDtypeStruct((rows, cols, channels), jnp.bfloat16),
        in_specs=[VMEM] * 7,
        out_specs=VMEM,
        scratch_shapes=[
            pltpu.VMEM((cols, padded, channels), jnp.bfloat16),
            pltpu.VMEM((cols, padded, channels), jnp.float32),
            pltpu.VMEM((2, owners, steps) + block, jnp.bfloat16),
            pltpu.VMEM((steps, 2, fellows) + block, jnp.bfloat16),
            pltpu.VMEM((steps, fellows) + block, jnp.bfloat16),
            pltpu.VMEM((steps, fellows) + block, jnp.bfloat16),
            pltpu.VMEM((owners, steps) + block, jnp.bfloat16),
        ]
        + [pltpu.SemaphoreType.DMA((steps,))] * 9,
        compiler_params=pltpu.CompilerParams(collective_id=0, has_side_effects=True, vmem_limit_bytes=VMEM_LIMIT),
        name="triangle",
    )(
        pair,
        pair_mask.T,
        ln_in_gain.reshape(1, 1, channels),
        proj_ab,
        gate_weight,
        ln_out_gain.reshape(1, hidden),
        out_weight,
    )


def solution(mesh):
    in_specs = (P("row", "col", None), P("row", "col"), P(), P(), P(), P(), P())
    out_specs = P("row", "col", None)
    return jax.shard_map(shards, mesh=mesh, in_specs=in_specs, out_specs=out_specs, check_vma=False)
```

```python
import functools

import jax
import jax.numpy as jnp
from jax import lax
from jax.experimental import pallas as pl
from jax.experimental.pallas import tpu as pltpu
from jax.sharding import PartitionSpec as P

EPS = 1e-05
LANES = 128
VMEM_LIMIT = 56 * 1024 * 1024
VMEM = pl.BlockSpec(memory_space=pltpu.VMEM)


def chunks(length, size):
    return [(at, min(at + size, length)) for at in range(0, length, size)]


def pad_rows(values, to):
    short = to - values.shape[-2]
    if short == 0:
        return values
    shape = values.shape[:-2] + (short, values.shape[-1])
    return jnp.concatenate([values, jnp.zeros(shape, values.dtype)], axis=-2)


def layer_norm(values, axis):
    middle = jnp.mean(values, axis=axis, keepdims=True)
    centred = values - middle
    spread = jnp.mean(centred * centred, axis=axis, keepdims=True)
    return centred * lax.rsqrt(spread + EPS)


def triangle_kernel(
    n_row, n_col, ends, pair_ref, mask_ref, in_gain_ref, proj_ref, gate_ref, out_gain_ref, weight_ref, update_ref,
    turned, gates, operands, left, right, product, landed, left_sent, left_came, far_sent, far_came, relay_sent, right_sent, right_came, back_sent, back_came,
):
    steps, _, fellows, per, cols, padded = left.shape
    rows, channels = pair_ref.shape[0], pair_ref.shape[2]
    hidden = weight_ref.shape[0]
    wide, quarter = n_col // 2, n_col // 4
    owners = n_row * quarter
    devices = n_row * n_col
    row, col = lax.axis_index("row"), lax.axis_index("col")
    half, spot = col // wide, lax.rem(col, wide)
    place, seat = spot // quarter, lax.rem(spot, quarter)
    middle = lax.rem(place + half, 2)
    mine, me = row * wide + spot, row * quarter + seat

    def owner_at(other, in_half, to_middle):
        shift = lax.rem(in_half + to_middle, 2) * quarter
        return other // quarter, in_half * wide + shift + lax.rem(other, quarter)

    barrier = pltpu.get_barrier_semaphore()

    def greet(offset, carry):
        other = lax.rem(row * n_col + col + offset, devices)
        device = other // n_col, lax.rem(other, n_col)
        pl.semaphore_signal(barrier, inc=1, device_id=device, device_id_type=pl.DeviceIdType.MESH)
        return carry

    lax.fori_loop(1, devices, greet, 0)

    for low, high in chunks(cols, 8):
        normed = layer_norm(pair_ref[:, low:high, :].astype(jnp.float32), -1) * in_gain_ref[...]
        turned[low:high] = pad_rows(jnp.transpose(normed, (1, 0, 2)), padded).astype(jnp.bfloat16)

    def make(side):
        weights = jnp.transpose(proj_ref[:, side * 2 * hidden : (side + 1) * 2 * hidden].astype(jnp.float32))
        weights = weights.astype(jnp.bfloat16)
        for low, high in chunks(cols, 8):
            rest = jnp.zeros((high - low, padded - rows), jnp.float32)
            valid = jnp.concatenate([mask_ref[low:high, :].astype(jnp.float32), rest], axis=1)
            each = []
            for at in range(low, high):
                projected = lax.dot_general(
                    weights, turned[at], (((1,), (1,)), ((), ())), preferred_element_type=jnp.float32
                )
                each.append(jax.nn.sigmoid(projected[:hidden]) * projected[hidden:] * valid[at - low : at - low + 1])
            each = jnp.transpose(jnp.stack(each), (1, 0, 2)).astype(jnp.bfloat16)
            operands[side, :, :, :, low:high, :] = each.reshape(owners, steps, per, high - low, padded)

    make(0)
    pl.semaphore_wait(barrier, devices - 1)

    def remote(source, target, sent, came, device):
        return pltpu.make_async_remote_copy(
            src_ref=source,
            dst_ref=target,
            send_sem=sent,
            recv_sem=came,
            device_id=device,
            device_id_type=pl.DeviceIdType.MESH,
        )

    def to_owners(source, target, sent, came, in_half, to_middle, skip):
        def one(offset, carry):
            other = lax.rem(me + offset, owners)
            remote(source(other), target, sent, came, owner_at(other, in_half, to_middle)).start()
            return carry

        lax.fori_loop(skip, owners, one, 0)

    def belongs(h):
        return middle if h >= ends else 1 - middle

    def send(side, h):
        target, sent, came = (left.at[h, half], left_sent, left_came) if side == 0 else (right.at[h], right_sent, right_came)
        member = belongs(h)

        @pl.when(member == 1)
        def _():
            pltpu.make_async_copy(operands.at[side, me, h], target.at[mine], came.at[h]).start()

        to_owners(lambda other: operands.at[side, other, h], target.at[mine], sent.at[h], came.at[h], half, int(h >= ends), member)

    def send_far(h):
        target = left.at[h, half, mine]
        to_owners(lambda other: operands.at[0, other, h], target, far_sent.at[h], far_came.at[h], 1 - half, 0, 0)

    send(0, ends)
    for h in range(ends):
        send_far(h)
    for h in range(ends + 1, steps):
        send(0, h)
    for h in range(ends):
        send(0, h)
    make(1)
    for h in range(steps):
        send(1, h)

    def open_gate(at, carry):
        gate = jnp.dot(turned[at], gate_ref[...], preferred_element_type=jnp.float32)
        gates[at] = jax.nn.sigmoid(gate)
        return carry

    lax.fori_loop(0, cols, open_gate, 0)

    def wait_for(ref, sem):
        pltpu.make_async_copy(ref, ref, sem).wait()

    def relay(h):
        return remote(
            left.at[h, half], left.at[h, half], relay_sent.at[h], far_came.at[h], (row, owner_at(me, 1 - half, 1)[1])
        )

    def pass_on(h):
        wait_for(left.at[h, half], left_came.at[h])
        relay(h).start()

    def channels(h):
        wait_for(right.at[h], right_came.at[h])
        wait_for(left.at[h, 1 - half], far_came.at[h])
        for p in range(per):
            firsts, seconds = [], []
            for at in range(n_row):
                span = slice(at * wide, (at + 1) * wide)
                both = [left[h, side, span, p].reshape(wide * cols, padded) for side in range(2)]
                firsts.append(jnp.concatenate(both, axis=0))
                seconds.append(right[h, span, p].reshape(wide * cols, padded))
            firsts, seconds = jnp.concatenate(firsts, axis=1), jnp.concatenate(seconds, axis=1)
            for at in range(n_row):
                panel = pad_rows(firsts[at * rows : (at + 1) * rows], padded)
                tri = lax.dot_general(seconds, panel, (((1,), (1,)), ((), ())), preferred_element_type=jnp.float32)
                product[h, at * wide : (at + 1) * wide, p] = tri.reshape(wide, cols, padded).astype(jnp.bfloat16)
        pltpu.make_async_copy(product.at[h, mine], landed.at[me, h], back_came.at[h]).start()

        def one(offset, carry):
            other = lax.rem(mine + offset, fellows)
            device = other // wide, half * wide + lax.rem(other, wide)
            remote(product.at[h, other], landed.at[me, h], back_sent.at[h], back_came.at[h], device).start()
            return carry

        lax.fori_loop(1, fellows, one, 0)

    ahead = steps - ends

    @pl.when(middle == 1)
    def _():
        for h in range(ends, ends + ahead):
            pass_on(h)

        def one(h, carry):
            pass_on(h + ahead)
            channels(h)
            return carry

        def last(h, carry):
            channels(h)
            return carry

        lax.fori_loop(ends, steps - ahead, one, 0)
        lax.fori_loop(steps - ahead, steps, last, 0)

    @pl.when(middle == 0)
    def _():
        def one(h, carry):
            wait_for(left.at[h, half], left_came.at[h])
            channels(h)
            return carry

        lax.fori_loop(0, ends, one, 0)

    for h in range(steps):
        member = belongs(h)
        wait_for(landed.at[:, h], back_came.at[h])
        if h < ends:
            wait_for(left.at[h, 0, pl.ds(0, owners)], far_sent.at[h])

        @pl.when(member == 1)
        def _():
            others = left.at[h, 0, pl.ds(0, owners - 1)]
            wait_for(others, left_sent.at[h])
            wait_for(others, right_sent.at[h])
            wait_for(product.at[h, pl.ds(0, fellows - 1)], back_sent.at[h])
            if h >= ends:
                wait_for(left.at[h, half], relay_sent.at[h])

        @pl.when(member == 0)
        def _():
            everyone = left.at[h, 0, pl.ds(0, owners)]
            wait_for(everyone, left_sent.at[h])
            wait_for(everyone, right_sent.at[h])

    out_gain = jnp.transpose(jnp.broadcast_to(out_gain_ref[...], (padded, hidden)))
    for low, high in chunks(cols, 8):
        tri = landed[:, :, :, low:high, :].astype(jnp.float32).reshape(hidden, high - low, padded)
        tri = (jnp.transpose(layer_norm(tri, 0), (1, 0, 2)) * out_gain).astype(jnp.bfloat16)
        mixed = []
        for at in range(low, high):
            mix = lax.dot_general(
                tri[at - low], weight_ref[...], (((0,), (0,)), ((), ())), preferred_element_type=jnp.float32
            )
            mixed.append((gates[at] * mix)[:rows])
        update_ref[low:high] = jnp.stack(mixed).astype(jnp.bfloat16)


def shards(pair, pair_mask, ln_in_gain, proj_ab, gate_weight, ln_out_gain, out_weight):
    rows, cols, channels = pair.shape
    hidden = out_weight.shape[0]
    n_row, n_col = lax.axis_size("row"), lax.axis_size("col")
    fellows = n_row * (n_col // 2)
    owners = n_row * (n_col // 4)
    part = hidden // owners
    per = max(part // 16, 1)
    steps = part // per
    ends = steps // 4
    padded = -(-rows // LANES) * LANES
    block = (per, cols, padded)
    return pl.pallas_call(
        functools.partial(triangle_kernel, n_row, n_col, ends),
        out_shape=jax.ShapeDtypeStruct((cols, rows, channels), jnp.bfloat16),
        in_specs=[VMEM] * 7,
        out_specs=VMEM,
        scratch_shapes=[
            pltpu.VMEM((cols, padded, channels), jnp.bfloat16),
            pltpu.VMEM((cols, padded, channels), jnp.float32),
            pltpu.VMEM((2, owners, steps) + block, jnp.bfloat16),
            pltpu.VMEM((steps, 2, fellows) + block, jnp.bfloat16),
            pltpu.VMEM((steps, fellows) + block, jnp.bfloat16),
            pltpu.VMEM((steps, fellows) + block, jnp.bfloat16),
            pltpu.VMEM((owners, steps) + block, jnp.bfloat16),
        ]
        + [pltpu.SemaphoreType.DMA((steps,))] * 9,
        compiler_params=pltpu.CompilerParams(collective_id=0, has_side_effects=True, vmem_limit_bytes=VMEM_LIMIT),
        name="triangle",
    )(
        pair,
        pair_mask.T,
        ln_in_gain.reshape(1, 1, channels),
        proj_ab,
        gate_weight,
        ln_out_gain.reshape(1, hidden),
        out_weight,
    ).transpose(1, 0, 2)


def solution(mesh):
    in_specs = (P("row", "col", None), P("row", "col"), P(), P(), P(), P(), P())
    out_specs = P("row", "col", None)
    return jax.shard_map(shards, mesh=mesh, in_specs=in_specs, out_specs=out_specs, check_vma=False)
```
